256 devices in a mesh: seq: 32 (over x_hi, z, core), batch: 8 (over x_lo, y).
Axes of the slice: x: 4 (x_hi: 2, x_lo: 2; x = x_hi * 2 + x_lo), y: 4, z: 8, core: 2. Of those that a mesh axis runs over, the one named last changes fastest.
Arguments:
- key_rows: bfloat16 [16384, 4096], P('seq', 'batch'), parts along dimension 1, may hold values from -6 to 6
- value_rows: bfloat16 [16384, 4096], P('seq', 'batch'), parts along dimension 1, may hold values from -6 to 6
- key_kernel: float32 [3, 4096], P(None, 'batch'), parts along dimension 1, may hold values from -3 to 3
- value_kernel: float32 [3, 4096], P(None, 'batch'), parts along dimension 1, may hold values from -3 to 3
- long_filter: bfloat16 [16384, 4096], P('seq', 'batch'), parts along dimension 1, may hold values from -0.046875 to 0.046875
- skip_gain: float32 [4096], P('batch'), parts along dimension 0, may hold values from 0.5 to 1.5
Outputs:
- filtered: bfloat16 [16384, 4096], P('seq', 'batch'), parts along dimension 1
The draws below stay inside these ranges and needn't reach their ends.
There are 8 independent parts, one for each index of `batch`. The reference program is written for one: setup_inputs(seed, part) draws one part's arguments, and reference() takes and returns one part's arrays. A program takes and returns all parts, laid end to end along the dimension named above; each array names one. Nothing has to cross between parts.
All inputs are finite; a program needn't handle non-finite values.
Results may differ from the reference program's by a relative error of at most 0.011.
Values may be sent and summed in bfloat16 or wider, within the bound.
A program may use at most 64 MiB of HBM per device.

```python
import jax
import jax.numpy as jnp

CH = 512
SEQ = 16384


def block_levels(stream_key, extent, cuts, smallest, high):
    loudness = 1.0
    for axis_at, shards_of in cuts:
        heights = jax.random.uniform(jax.random.fold_in(jax.random.fold_in(stream_key, 6), axis_at), (shards_of,), jnp.float32, smallest / len(cuts), high / len(cuts))
        loudness = loudness * jnp.repeat(jnp.exp(heights), extent[axis_at] // shards_of).reshape((-1,) + (1,) * (len(extent) - 1 - axis_at))
    return loudness


def bell_draw(stream_key, shape, scale, reach, cuts=(), held_as=jnp.bfloat16):
    factor_of = block_levels(stream_key, shape, cuts, -0.22, 0.18) if cuts else 1.0
    array = jax.random.normal(stream_key, shape, jnp.float32) * scale * factor_of
    return jnp.minimum(jnp.maximum(array, -reach), reach).astype(held_as)


def setup_inputs(seed: int = 0, part: int = 0) -> dict:
    seeds = jax.random.split(jax.random.key(seed), 7)
    part_splits = jax.random.split(jax.random.fold_in(seeds[6], part), 7)
    key_rows = bell_draw(part_splits[0], (SEQ, CH), 1.0, 6.0, ((0, 32),))
    value_rows = bell_draw(part_splits[1], (SEQ, CH), 1.0, 6.0, ((0, 32),))
    key_kernel = bell_draw(part_splits[2], (3, CH), 0.6, 3.0, (), jnp.float32)
    value_kernel = bell_draw(part_splits[3], (3, CH), 0.6, 3.0, (), jnp.float32)
    long_filter = bell_draw(part_splits[4], (SEQ, CH), SEQ ** -0.5, 0.046875, ((0, 32),))
    skip_gain = jnp.clip(jax.random.uniform(part_splits[5], (CH,), jnp.float32, 0.5, 1.5), 0.5, 1.5)
    return dict(key_rows=key_rows, value_rows=value_rows, key_kernel=key_kernel, value_kernel=value_kernel, long_filter=long_filter, skip_gain=skip_gain)


def short_filter(samples, kernel):
    padded = jnp.concatenate([jnp.zeros((2, CH), samples.dtype), samples], axis=0).astype(jnp.float32)
    return kernel[0] * padded[2:] + kernel[1] * padded[1:SEQ + 1] + kernel[2] * padded[:SEQ]


def reference(key_rows, value_rows, key_kernel, value_kernel, long_filter, skip_gain):
    short_keys = short_filter(key_rows, key_kernel)
    short_values = short_filter(value_rows, value_kernel)
    gated_rows = (short_keys * short_values).astype(jnp.bfloat16)
    signal = gated_rows.astype(jnp.float32)
    spectra = jnp.fft.rfft(signal, n=2 * SEQ, axis=0) * jnp.fft.rfft(long_filter.astype(jnp.float32), n=2 * SEQ, axis=0)
    convolved = jnp.fft.irfft(spectra, n=2 * SEQ, axis=0)[:SEQ]
    return (convolved + skip_gain * signal).astype(jnp.bfloat16)
```

```python
import functools
import math

import jax
import jax.numpy as jnp
import numpy as np
from jax import lax
from jax.experimental import pallas as pl
from jax.experimental.pallas import tpu as pltpu
from jax.sharding import PartitionSpec as P

import ml_dtypes

MESH = pl.DeviceIdType.MESH
F32 = jnp.float32
BF16 = jnp.bfloat16
CHUNKS = 2
LANES = 8
HALVES = 2


def tables(n, rows):
    length = n * rows
    half = rows // HALVES
    outer = 2.0 * math.pi * np.outer(np.arange(n) + 0.25, np.arange(n)) / n
    pair = np.stack([np.cos(outer), -np.sin(outer)])
    first = np.einsum("pks,hg,cd->hpcksgd", pair, np.eye(HALVES), np.eye(LANES))
    first = first.reshape(HALVES, 2 * LANES * n, n * HALVES * LANES)
    last = first.reshape(-1, first.shape[-1]).T
    inner = 2.0 * math.pi * (np.outer(np.arange(rows), np.arange(rows)) % rows) / rows
    c, s = np.cos(inner), np.sin(inner)
    middle = np.block([[c, -s], [s, c]])
    twist = 2.0 * math.pi * np.outer(np.arange(n) + 0.25, np.arange(rows)) / length
    low = lambda a: np.ascontiguousarray(a).astype(ml_dtypes.bfloat16)
    return (
        low(first),
        low(last),
        low(middle),
        np.stack([np.cos(twist), np.sin(twist)]).astype(np.float32),
    )


def kernel(
    n,
    key_hbm,
    value_hbm,
    key_kernel,
    value_kernel,
    filter_hbm,
    skip,
    first_hbm,
    last_hbm,
    middle_hbm,
    twist_hbm,
    out_hbm,
    keys,
    values,
    filt,
    first,
    last,
    middle,
    twist,
    rim,
    send,
    recv,
    spectrum,
    mixed,
    stacked,
    out,
    in_sem,
    rim_send,
    rim_recv,
    send_sem,
    recv_sem,
    out_sem,
):
    me = lax.axis_index("seq")
    rows, channels = keys.shape
    half = rows // HALVES
    width = channels // CHUNKS
    modes = LANES * n
    right = lax.rem(me + 1, n)

    loads = [
        pltpu.make_async_copy(source, target, in_sem.at[i])
        for i, (source, target) in enumerate(
            (
                (filter_hbm, filt),
                (key_hbm, keys),
                (value_hbm, values),
                (first_hbm, first),
                (twist_hbm, twist),
                (middle_hbm, middle),
                (last_hbm, last),
            )
        )
    ]
    for load in loads:
        load.start()

    barrier = pltpu.get_barrier_semaphore()

    def greet(p, carry):
        pl.semaphore_signal(
            barrier, inc=1, device_id={"seq": lax.rem(me + p, n)}, device_id_type=MESH
        )
        return carry

    lax.fori_loop(1, n, greet, 0)

    def pack(slot, block):
        turned = jnp.transpose(block.astype(F32))
        parts = [
            turned[:, h * half : (h + 1) * half].reshape(n, 1, LANES, half)
            for h in range(HALVES)
        ]
        slabs = jnp.concatenate(parts, axis=1).reshape(n, HALVES * LANES, half)
        send[slot] = slabs.astype(BF16)

    def scatter(slot):
        def step(p, carry):
            peer = lax.rem(me + p, n)
            pltpu.make_async_remote_copy(
                src_ref=send.at[slot, peer],
                dst_ref=recv.at[slot, me],
                send_sem=send_sem.at[slot],
                recv_sem=recv_sem.at[slot],
                device_id={"seq": peer},
                device_id_type=MESH,
            ).start()
            return carry

        lax.fori_loop(1, n, step, 0)
        recv[slot, pl.ds(me, 1)] = send[slot, pl.ds(me, 1)]

    def arrived(slot):
        block = recv.at[slot, pl.ds(0, n - 1)]
        pltpu.make_async_copy(block, block, recv_sem.at[slot]).wait()

    def gone(slot):
        block = send.at[slot, pl.ds(0, n - 1)]
        pltpu.make_async_copy(block, block, send_sem.at[slot]).wait()

    def turn(part, h):
        table = twist[part, :, h * half : (h + 1) * half]
        return jnp.broadcast_to(table[None], (LANES, n, half)).reshape(modes, half)

    def forward(slot):
        block = recv[slot].reshape(n * HALVES * LANES, half)
        for h in range(HALVES):
            both = jnp.dot(first[h], block, preferred_element_type=F32)
            re, im = both[:modes], both[modes:]
            c, s = turn(0, h), turn(1, h)
            mixed[:, h * half : (h + 1) * half] = (re * c + im * s).astype(BF16)
            mixed[:, rows + h * half : rows + (h + 1) * half] = (im * c - re * s).astype(BF16)
        return (
            jnp.dot(mixed[...], middle[:, :rows], preferred_element_type=F32),
            jnp.dot(mixed[...], middle[:, rows:], preferred_element_type=F32),
        )

    loads[0].wait()
    pack(0, filt[:, :width])
    pl.semaphore_wait(barrier, n - 1)
    loads[1].wait()
    loads[2].wait()
    rims = [
        pltpu.make_async_remote_copy(
            src_ref=array.at[pl.ds(rows - 16, 16)],
            dst_ref=rim.at[i],
            send_sem=rim_send.at[i],
            recv_sem=rim_recv.at[i],
            device_id={"seq": right},
            device_id_type=MESH,
        )
        for i, array in enumerate((keys, values))
    ]
    for copy in rims:
        copy.start()
    scatter(0)
    pack(1, filt[:, width:])
    scatter(1)
    for copy in rims:
        copy.wait_recv()

    def short(samples, i, taps, columns):
        behind = rim[i, :, columns].astype(F32) * (me > 0).astype(F32)
        longer = jnp.concatenate([behind[8:], samples[:, columns].astype(F32)], axis=0)
        return (
            taps[0:1, columns] * longer[8:]
            + taps[1:2, columns] * longer[7 : rows + 7]
            + taps[2:3, columns] * longer[6 : rows + 6]
        )

    for q in range(CHUNKS):
        columns = slice(q * width, (q + 1) * width)
        gated = short(keys, 0, key_kernel, columns) * short(values, 1, value_kernel, columns)
        pack(2 + q, gated.astype(BF16))
        scatter(2 + q)

    for load in loads[3:]:
        load.wait()
    scale = 1.0 / (n * rows)
    for q in range(CHUNKS):
        arrived(q)
        re, im = forward(q)
        for c in range(LANES):
            gain = skip[q * width + me * LANES + c]
            spectrum[q, 0, c * n : (c + 1) * n] = (re[c * n : (c + 1) * n] + gain) * scale
        spectrum[q, 1] = im * scale

    for q in range(CHUNKS):
        arrived(2 + q)
        re, im = forward(2 + q)
        fre, fim = spectrum[q, 0], spectrum[q, 1]
        mixed[:, :rows] = (re * fim + im * fre).astype(BF16)
        mixed[:, rows:] = (re * fre - im * fim).astype(BF16)
        im = jnp.dot(mixed[...], middle[:, :rows], preferred_element_type=F32)
        re = jnp.dot(mixed[...], middle[:, rows:], preferred_element_type=F32)
        for h in range(HALVES):
            part = slice(h * half, (h + 1) * half)
            c, s = turn(0, h), turn(1, h)
            start = 2 * h * modes
            stacked[start : start + modes] = (re[:, part] * c - im[:, part] * s).astype(BF16)
            stacked[start + modes : start + 2 * modes] = (
                im[:, part] * c + re[:, part] * s
            ).astype(BF16)
        done = jnp.dot(last[...], stacked[...], preferred_element_type=F32)
        send[4 + q] = done.astype(BF16).reshape(n, HALVES * LANES, half)
        scatter(4 + q)

    stores = []
    for q in range(CHUNKS):
        arrived(4 + q)
        block = recv[4 + q].astype(F32).reshape(n, HALVES, LANES, half)
        columns = slice(q * width, (q + 1) * width)
        for h in range(HALVES):
            piece = block[:, h].reshape(width, half)
            out[h * half : (h + 1) * half, columns] = jnp.transpose(piece).astype(BF16)
        store = pltpu.make_async_copy(
            out.at[:, columns], out_hbm.at[:, columns], out_sem.at[q]
        )
        store.start()
        stores.append(store)

    for copy in rims:
        copy.wait_send()
    for slot in range(3 * CHUNKS):
        gone(slot)
    for store in stores:
        store.wait()


def on_device(n, key_rows, value_rows, key_kernel, value_kernel, long_filter, skip_gain):
    rows, channels = key_rows.shape
    half = rows // HALVES
    modes = LANES * n
    first, last, middle, twist = tables(n, rows)
    vmem = pl.BlockSpec(memory_space=pltpu.VMEM)
    smem = pl.BlockSpec(memory_space=pltpu.SMEM)
    hbm = pl.BlockSpec(memory_space=pl.ANY)
    slabs = (3 * CHUNKS, n, HALVES * LANES, half)
    return pl.pallas_call(
        functools.partial(kernel, n),
        out_shape=jax.ShapeDtypeStruct((rows, channels), BF16),
        in_specs=[hbm, hbm, vmem, vmem, hbm, smem, hbm, hbm, hbm, hbm],
        out_specs=hbm,
        scratch_shapes=[
            pltpu.VMEM((rows, channels), BF16),
            pltpu.VMEM((rows, channels), BF16),
            pltpu.VMEM((rows, channels), BF16),
            pltpu.VMEM(first.shape, BF16),
            pltpu.VMEM(last.shape, BF16),
            pltpu.VMEM(middle.shape, BF16),
            pltpu.VMEM(twist.shape, F32),
            pltpu.VMEM((2, 16, channels), BF16),
            pltpu.VMEM(slabs, BF16),
            pltpu.VMEM(slabs, BF16),
            pltpu.VMEM((CHUNKS, 2, modes, rows), F32),
            pltpu.VMEM((modes, 2 * rows), BF16),
            pltpu.VMEM((2 * HALVES * modes, half), BF16),
            pltpu.VMEM((rows, channels), BF16),
            pltpu.SemaphoreType.DMA((7,)),
            pltpu.SemaphoreType.DMA((2,)),
            pltpu.SemaphoreType.DMA((2,)),
            pltpu.SemaphoreType.DMA((3 * CHUNKS,)),
            pltpu.SemaphoreType.DMA((3 * CHUNKS,)),
            pltpu.SemaphoreType.DMA((CHUNKS,)),
        ],
        compiler_params=pltpu.CompilerParams(
            collective_id=0, has_side_effects=True, vmem_limit_bytes=40 * 1024 * 1024
        ),
    )(
        key_rows,
        value_rows,
        key_kernel,
        value_kernel,
        long_filter,
        skip_gain,
        jnp.asarray(first),
        jnp.asarray(last),
        jnp.asarray(middle),
        jnp.asarray(twist),
    )


def solution(mesh):
    return jax.shard_map(
        functools.partial(on_device, mesh.shape["seq"]),
        mesh=mesh,
        in_specs=(
            P("seq", "batch"),
            P("seq", "batch"),
            P(None, "batch"),
            P(None, "batch"),
            P("seq", "batch"),
            P("batch"),
        ),
        out_specs=P("seq", "batch"),
        check_vma=False,
    )
```

```python
import functools
import math

import jax
import jax.numpy as jnp
import numpy as np
from jax import lax
from jax.experimental import pallas as pl
from jax.experimental.pallas import tpu as pltpu
from jax.sharding import PartitionSpec as P

import ml_dtypes

MESH = pl.DeviceIdType.MESH
F32 = jnp.float32
BF16 = jnp.bfloat16
CHUNKS = 2
LANES = 8
HALVES = 2


def tables(n, rows):
    length = n * rows
    half = rows // HALVES
    outer = 2.0 * math.pi * np.outer(np.arange(n) + 0.25, np.arange(n)) / n
    pair = np.stack([np.cos(outer), -np.sin(outer)])
    first = np.einsum("pks,hg,cd->hpcksgd", pair, np.eye(HALVES), np.eye(LANES))
    first = first.reshape(HALVES, 2 * LANES * n, n * HALVES * LANES)
    last = first.reshape(-1, first.shape[-1]).T
    inner = 2.0 * math.pi * (np.outer(np.arange(rows), np.arange(rows)) % rows) / rows
    c, s = np.cos(inner), np.sin(inner)
    middle = np.block([[c, -s], [s, c]])
    twist = 2.0 * math.pi * np.outer(np.arange(n) + 0.25, np.arange(rows)) / length
    low = lambda a: np.ascontiguousarray(a).astype(ml_dtypes.bfloat16)
    return (
        low(first),
        low(last),
        low(middle),
        np.stack([np.cos(twist), np.sin(twist)]).astype(np.float32),
    )


def kernel(
    n,
    key_hbm,
    value_hbm,
    key_kernel,
    value_kernel,
    filter_hbm,
    skip,
    first_hbm,
    last_hbm,
    middle_hbm,
    twist_hbm,
    out,
    keys,
    values,
    filt,
    first,
    last,
    middle,
    twist,
    rim,
    send,
    recv,
    spectrum,
    mixed,
    stacked,
    in_sem,
    rim_send,
    rim_recv,
    send_sem,
    recv_sem,
):
    me = lax.axis_index("seq")
    rows, channels = keys.shape
    half = rows // HALVES
    width = channels // CHUNKS
    modes = LANES * n
    right = lax.rem(me + 1, n)

    barrier = pltpu.get_barrier_semaphore()

    def greet(p, carry):
        pl.semaphore_signal(
            barrier, inc=1, device_id={"seq": lax.rem(me + p, n)}, device_id_type=MESH
        )
        return carry

    lax.fori_loop(1, n, greet, 0)

    loads = [
        pltpu.make_async_copy(source, target, in_sem.at[i])
        for i, (source, target) in enumerate(
            (
                (filter_hbm, filt),
                (key_hbm, keys),
                (value_hbm, values),
                (first_hbm, first),
                (twist_hbm, twist),
                (middle_hbm, middle),
                (last_hbm, last),
            )
        )
    ]
    for load in loads:
        load.start()

    def pack(slot, block):
        turned = jnp.transpose(block.astype(F32))
        parts = [
            turned[:, h * half : (h + 1) * half].reshape(n, 1, LANES, half)
            for h in range(HALVES)
        ]
        slabs = jnp.concatenate(parts, axis=1).reshape(n, HALVES * LANES, half)
        send[slot] = slabs.astype(BF16)

    def scatter(slot):
        def step(p, carry):
            peer = lax.rem(me + p, n)
            pltpu.make_async_remote_copy(
                src_ref=send.at[slot, peer],
                dst_ref=recv.at[slot, me],
                send_sem=send_sem.at[slot],
                recv_sem=recv_sem.at[slot],
                device_id={"seq": peer},
                device_id_type=MESH,
            ).start()
            return carry

        lax.fori_loop(1, n, step, 0)
        recv[slot, pl.ds(me, 1)] = send[slot, pl.ds(me, 1)]

    def arrived(slot):
        block = recv.at[slot, pl.ds(0, n - 1)]
        pltpu.make_async_copy(block, block, recv_sem.at[slot]).wait()

    def gone(slot):
        block = send.at[slot, pl.ds(0, n - 1)]
        pltpu.make_async_copy(block, block, send_sem.at[slot]).wait()

    def turn(part, h):
        table = twist[part, :, h * half : (h + 1) * half]
        return jnp.broadcast_to(table[None], (LANES, n, half)).reshape(modes, half)

    def forward(slot):
        block = recv[slot].reshape(n * HALVES * LANES, half)
        for h in range(HALVES):
            both = jnp.dot(first[h], block, preferred_element_type=F32)
            re, im = both[:modes], both[modes:]
            c, s = turn(0, h), turn(1, h)
            mixed[:, h * half : (h + 1) * half] = (re * c + im * s).astype(BF16)
            mixed[:, rows + h * half : rows + (h + 1) * half] = (im * c - re * s).astype(BF16)
        return (
            jnp.dot(mixed[...], middle[:, :rows], preferred_element_type=F32),
            jnp.dot(mixed[...], middle[:, rows:], preferred_element_type=F32),
        )

    loads[0].wait()
    pack(0, filt[:, :width])
    pl.semaphore_wait(barrier, n - 1)
    loads[1].wait()
    loads[2].wait()
    rims = [
        pltpu.make_async_remote_copy(
            src_ref=array.at[pl.ds(rows - 16, 16)],
            dst_ref=rim.at[i],
            send_sem=rim_send.at[i],
            recv_sem=rim_recv.at[i],
            device_id={"seq": right},
            device_id_type=MESH,
        )
        for i, array in enumerate((keys, values))
    ]
    for copy in rims:
        copy.start()
    scatter(0)
    pack(1, filt[:, width:])
    for copy in rims:
        copy.wait_recv()

    def short(samples, i, taps, columns):
        behind = rim[i, :, columns].astype(F32) * (me > 0).astype(F32)
        longer = jnp.concatenate([behind[8:], samples[:, columns].astype(F32)], axis=0)
        return (
            taps[0:1, columns] * longer[8:]
            + taps[1:2, columns] * longer[7 : rows + 7]
            + taps[2:3, columns] * longer[6 : rows + 6]
        )

    for q in range(CHUNKS):
        columns = slice(q * width, (q + 1) * width)
        gated = short(keys, 0, key_kernel, columns) * short(values, 1, value_kernel, columns)
        pack(2 + q, gated.astype(BF16))
        scatter(2 + q)
        if q == 0:
            scatter(1)

    for load in loads[3:]:
        load.wait()
    scale = 1.0 / (n * rows)
    for q in range(CHUNKS):
        arrived(q)
        re, im = forward(q)
        for c in range(LANES):
            gain = skip[q * width + me * LANES + c]
            spectrum[q, 0, c * n : (c + 1) * n] = (re[c * n : (c + 1) * n] + gain) * scale
        spectrum[q, 1] = im * scale

    for q in range(CHUNKS):
        arrived(2 + q)
        re, im = forward(2 + q)
        fre, fim = spectrum[q, 0], spectrum[q, 1]
        mixed[:, :rows] = (re * fim + im * fre).astype(BF16)
        mixed[:, rows:] = (re * fre - im * fim).astype(BF16)
        im = jnp.dot(mixed[...], middle[:, :rows], preferred_element_type=F32)
        re = jnp.dot(mixed[...], middle[:, rows:], preferred_element_type=F32)
        for h in range(HALVES):
            part = slice(h * half, (h + 1) * half)
            c, s = turn(0, h), turn(1, h)
            start = 2 * h * modes
            stacked[start : start + modes] = (re[:, part] * c - im[:, part] * s).astype(BF16)
            stacked[start + modes : start + 2 * modes] = (
                im[:, part] * c + re[:, part] * s
            ).astype(BF16)
        done = jnp.dot(last[...], stacked[...], preferred_element_type=F32)
        send[4 + q] = done.astype(BF16).reshape(n, HALVES * LANES, half)
        scatter(4 + q)

    for q in range(CHUNKS):
        arrived(4 + q)
        block = recv[4 + q].astype(F32).reshape(n, HALVES, LANES, half)
        columns = slice(q * width, (q + 1) * width)
        for h in range(HALVES):
            piece = block[:, h].reshape(width, half)
            out[h * half : (h + 1) * half, columns] = jnp.transpose(piece).astype(BF16)

    for copy in rims:
        copy.wait_send()
    for slot in range(3 * CHUNKS):
        gone(slot)


def on_device(n, key_rows, value_rows, key_kernel, value_kernel, long_filter, skip_gain):
    rows, channels = key_rows.shape
    half = rows // HALVES
    modes = LANES * n
    first, last, middle, twist = tables(n, rows)
    vmem = pl.BlockSpec(memory_space=pltpu.VMEM)
    smem = pl.BlockSpec(memory_space=pltpu.SMEM)
    hbm = pl.BlockSpec(memory_space=pltpu.HBM)
    slabs = (3 * CHUNKS, n, HALVES * LANES, half)
    return pl.pallas_call(
        functools.partial(kernel, n),
        out_shape=pltpu.VMEM((rows, channels), BF16),
        in_specs=[hbm, hbm, vmem, vmem, hbm, smem, hbm, hbm, hbm, hbm],
        out_specs=vmem,
        scratch_shapes=[
            pltpu.VMEM((rows, channels), BF16),
            pltpu.VMEM((rows, channels), BF16),
            pltpu.VMEM((rows, channels), BF16),
            pltpu.VMEM(first.shape, BF16),
            pltpu.VMEM(last.shape, BF16),
            pltpu.VMEM(middle.shape, BF16),
            pltpu.VMEM(twist.shape, F32),
            pltpu.VMEM((2, 16, channels), BF16),
            pltpu.VMEM(slabs, BF16),
            pltpu.VMEM(slabs, BF16),
            pltpu.VMEM((CHUNKS, 2, modes, rows), F32),
            pltpu.VMEM((modes, 2 * rows), BF16),
            pltpu.VMEM((2 * HALVES * modes, half), BF16),
            pltpu.SemaphoreType.DMA((7,)),
            pltpu.SemaphoreType.DMA((2,)),
            pltpu.SemaphoreType.DMA((2,)),
            pltpu.SemaphoreType.DMA((3 * CHUNKS,)),
            pltpu.SemaphoreType.DMA((3 * CHUNKS,)),
        ],
        compiler_params=pltpu.CompilerParams(
            collective_id=0, has_side_effects=True, vmem_limit_bytes=63 * 1024 * 1024
        ),
    )(
        key_rows,
        value_rows,
        key_kernel,
        value_kernel,
        long_filter,
        skip_gain,
        jnp.asarray(first),
        jnp.asarray(last),
        jnp.asarray(middle),
        jnp.asarray(twist),
    )


def solution(mesh):
    return jax.shard_map(
        functools.partial(on_device, mesh.shape["seq"]),
        mesh=mesh,
        in_specs=(
            P("seq", "batch"),
            P("seq", "batch"),
            P(None, "batch"),
            P(None, "batch"),
            P("seq", "batch"),
            P("batch"),
        ),
        out_specs=P("seq", "batch"),
        check_vma=False,
    )
```

```python
import functools
import math

import jax
import jax.numpy as jnp
import numpy as np
from jax import lax
from jax.experimental import pallas as pl
from jax.experimental.pallas import tpu as pltpu
from jax.sharding import PartitionSpec as P

import ml_dtypes

MESH = pl.DeviceIdType.MESH
F32 = jnp.float32
BF16 = jnp.bfloat16
CHUNKS = 4
LANES = 4
PIECES = 4


def tables(n, rows):
    length = n * rows
    piece_rows = rows // PIECES
    outer = 2.0 * math.pi * np.outer(np.arange(n) + 0.25, np.arange(n)) / n
    pair = np.stack([np.cos(outer), -np.sin(outer)])
    first = np.einsum("pks,hg,cd->hpcksgd", pair, np.eye(PIECES), np.eye(LANES))
    first = first.reshape(PIECES * 2 * LANES * n, n * PIECES * LANES)
    last = first.T
    inner = 2.0 * math.pi * (np.outer(np.arange(rows), np.arange(rows)) % rows) / rows
    c, s = np.cos(inner), np.sin(inner)
    middle = np.block([[c, -s], [s, c]])
    order = np.einsum("de,hg,cb->dhcgeb", np.eye(n), np.eye(PIECES), np.eye(LANES))
    order = order.reshape(n * PIECES * LANES, -1)
    twist = 2.0 * math.pi * np.outer(np.arange(n) + 0.25, np.arange(rows)) / length
    low = lambda a: np.ascontiguousarray(a).astype(ml_dtypes.bfloat16)
    return (
        low(first),
        low(last),
        low(middle),
        low(order),
        np.stack([np.cos(twist), np.sin(twist)]).astype(np.float32),
    )


def kernel(
    n,
    key_hbm,
    value_hbm,
    key_kernel,
    value_kernel,
    filter_hbm,
    skip,
    first_hbm,
    last_hbm,
    middle_hbm,
    order_hbm,
    twist_hbm,
    out,
    keys,
    values,
    filt,
    first,
    last,
    middle,
    order,
    twist,
    rim,
    send,
    recv,
    spectrum,
    mixed,
    stacked,
    in_sem,
    rim_send,
    rim_recv,
    send_sem,
    recv_sem,
):
    me = lax.axis_index("seq")
    planes = n // 4
    my_side, my_plane, my_core = me // (2 * planes), (me // 2) % planes, me % 2
    rows, channels = keys.shape
    piece_rows = rows // PIECES
    width = channels // CHUNKS
    modes = LANES * n
    right = lax.rem(me + 1, n)

    barrier = pltpu.get_barrier_semaphore()

    def greet(p, carry):
        pl.semaphore_signal(
            barrier, inc=1, device_id={"seq": lax.rem(me + p, n)}, device_id_type=MESH
        )
        return carry

    lax.fori_loop(1, n, greet, 0)

    loads = [
        pltpu.make_async_copy(source, target, in_sem.at[i])
        for i, (source, target) in enumerate(
            (
                (filter_hbm, filt),
                (order_hbm, order),
                (key_hbm, keys),
                (value_hbm, values),
                (first_hbm, first),
                (twist_hbm, twist),
                (middle_hbm, middle),
                (last_hbm, last),
            )
        )
    ]
    for load in loads:
        load.start()

    def pack(slot, block):
        parts = [block[h * piece_rows : (h + 1) * piece_rows] for h in range(PIECES)]
        slabs = lax.dot_general(
            order[...],
            jnp.concatenate(parts, axis=1),
            (((1,), (1,)), ((), ())),
            preferred_element_type=F32,
        )
        send[slot] = slabs.astype(BF16).reshape(n, PIECES * LANES, piece_rows)

    def flip(place, other):
        return 1 - place if other else place

    def send_to(slot, peer):
        pltpu.make_async_remote_copy(
            src_ref=send.at[slot, peer],
            dst_ref=recv.at[slot, me],
            send_sem=send_sem.at[slot],
            recv_sem=recv_sem.at[slot],
            device_id={"seq": peer},
            device_id_type=MESH,
        ).start()

    def scatter(slot):
        def step(i, carry):
            shift = (i + 1) // 2
            distance = planes // 2 + jnp.where(i % 2 == 1, -shift, shift)
            plane = my_plane + distance
            plane = jnp.where(plane >= planes, plane - planes, plane)
            for side in (1, 0):
                for core in (1, 0):
                    send_to(slot, flip(my_side, side) * 2 * planes + plane * 2 + flip(my_core, core))
            return carry

        lax.fori_loop(0, planes - 1, step, 0)
        for side, core in ((1, 1), (1, 0), (0, 1)):
            send_to(slot, flip(my_side, side) * 2 * planes + my_plane * 2 + flip(my_core, core))
        recv[slot, pl.ds(me, 1)] = send[slot, pl.ds(me, 1)]

    def arrived(slot):
        block = recv.at[slot, pl.ds(0, n - 1)]
        pltpu.make_async_copy(block, block, recv_sem.at[slot]).wait()

    def gone(slot):
        block = send.at[slot, pl.ds(0, n - 1)]
        pltpu.make_async_copy(block, block, send_sem.at[slot]).wait()

    def turn(part, h):
        table = twist[part, :, h * piece_rows : (h + 1) * piece_rows]
        return jnp.broadcast_to(table[None], (LANES, n, piece_rows)).reshape(modes, piece_rows)

    def forward(slot):
        block = recv[slot].reshape(n * PIECES * LANES, piece_rows)
        both = jnp.dot(first[...], block, preferred_element_type=F32)
        for h in range(PIECES):
            start = 2 * h * modes
            re, im = both[start : start + modes], both[start + modes : start + 2 * modes]
            c, s = turn(0, h), turn(1, h)
            mixed[:, h * piece_rows : (h + 1) * piece_rows] = (re * c + im * s).astype(BF16)
            mixed[:, rows + h * piece_rows : rows + (h + 1) * piece_rows] = (
                im * c - re * s
            ).astype(BF16)
        both = jnp.dot(mixed[...], middle[...], preferred_element_type=F32)
        return both[:, :rows], both[:, rows:]

    loads[0].wait()
    loads[1].wait()
    pack(0, filt[:, :width])
    pl.semaphore_wait(barrier, n - 1)
    loads[2].wait()
    loads[3].wait()
    rims = [
        pltpu.make_async_remote_copy(
            src_ref=array.at[pl.ds(rows - 16, 16)],
            dst_ref=rim.at[i],
            send_sem=rim_send.at[i],
            recv_sem=rim_recv.at[i],
            device_id={"seq": right},
            device_id_type=MESH,
        )
        for i, array in enumerate((keys, values))
    ]
    for copy in rims:
        copy.start()
    scatter(0)
    for copy in rims:
        copy.wait_recv()

    def short(samples, i, taps, columns):
        behind = rim[i, :, columns].astype(F32) * (me > 0).astype(F32)
        longer = jnp.concatenate([behind[8:], samples[:, columns].astype(F32)], axis=0)
        return (
            taps[0:1, columns] * longer[8:]
            + taps[1:2, columns] * longer[7 : rows + 7]
            + taps[2:3, columns] * longer[6 : rows + 6]
        )

    for q in range(CHUNKS):
        columns = slice(q * width, (q + 1) * width)
        if q:
            pack(q, filt[:, columns])
            scatter(q)
        gated = short(keys, 0, key_kernel, columns) * short(values, 1, value_kernel, columns)
        pack(CHUNKS + q, gated.astype(BF16))
        scatter(CHUNKS + q)

    for load in loads[4:]:
        load.wait()
    scale = 1.0 / (n * rows)
    for q in range(CHUNKS):
        arrived(q)
        re, im = forward(q)
        for c in range(LANES):
            gain = skip[q * width + me * LANES + c]
            spectrum[0, c * n : (c + 1) * n] = (re[c * n : (c + 1) * n] + gain) * scale
        spectrum[1] = im * scale

        arrived(CHUNKS + q)
        re, im = forward(CHUNKS + q)
        fre, fim = spectrum[0], spectrum[1]
        mixed[:, :rows] = (re * fim + im * fre).astype(BF16)
        mixed[:, rows:] = (re * fre - im * fim).astype(BF16)
        both = jnp.dot(mixed[...], middle[...], preferred_element_type=F32)
        im, re = both[:, :rows], both[:, rows:]
        for h in range(PIECES):
            part = slice(h * piece_rows, (h + 1) * piece_rows)
            c, s = turn(0, h), turn(1, h)
            start = 2 * h * modes
            stacked[start : start + modes] = (re[:, part] * c - im[:, part] * s).astype(BF16)
            stacked[start + modes : start + 2 * modes] = (
                im[:, part] * c + re[:, part] * s
            ).astype(BF16)
        done = jnp.dot(last[...], stacked[...], preferred_element_type=F32)
        send[2 * CHUNKS + q] = done.astype(BF16).reshape(n, PIECES * LANES, piece_rows)
        scatter(2 * CHUNKS + q)

    for q in range(CHUNKS):
        arrived(2 * CHUNKS + q)
        block = recv[2 * CHUNKS + q].reshape(n * PIECES * LANES, piece_rows)
        turned = lax.dot_general(
            block, order[...], (((0,), (0,)), ((), ())), preferred_element_type=F32
        )
        for h in range(PIECES):
            out[h * piece_rows : (h + 1) * piece_rows, q * width : (q + 1) * width] = turned[
                :, h * width : (h + 1) * width
            ].astype(BF16)

    for copy in rims:
        copy.wait_send()
    for slot in range(3 * CHUNKS):
        gone(slot)


def on_device(n, key_rows, value_rows, key_kernel, value_kernel, long_filter, skip_gain):
    rows, channels = key_rows.shape
    piece_rows = rows // PIECES
    modes = LANES * n
    first, last, middle, order, twist = tables(n, rows)
    vmem = pl.BlockSpec(memory_space=pltpu.VMEM)
    smem = pl.BlockSpec(memory_space=pltpu.SMEM)
    hbm = pl.BlockSpec(memory_space=pltpu.HBM)
    slabs = (3 * CHUNKS, n, PIECES * LANES, piece_rows)
    return pl.pallas_call(
        functools.partial(kernel, n),
        out_shape=pltpu.VMEM((rows, channels), BF16),
        in_specs=[hbm, hbm, vmem, vmem, hbm, smem, hbm, hbm, hbm, hbm, hbm],
        out_specs=vmem,
        scratch_shapes=[
            pltpu.VMEM((rows, channels), BF16),
            pltpu.VMEM((rows, channels), BF16),
            pltpu.VMEM((rows, channels), BF16),
            pltpu.VMEM(first.shape, BF16),
            pltpu.VMEM(last.shape, BF16),
            pltpu.VMEM(middle.shape, BF16),
            pltpu.VMEM(order.shape, BF16),
            pltpu.VMEM(twist.shape, F32),
            pltpu.VMEM((2, 16, channels), BF16),
            pltpu.VMEM(slabs, BF16),
            pltpu.VMEM(slabs, BF16),
            pltpu.VMEM((2, modes, rows), F32),
            pltpu.VMEM((modes, 2 * rows), BF16),
            pltpu.VMEM((2 * PIECES * modes, piece_rows), BF16),
            pltpu.SemaphoreType.DMA((8,)),
            pltpu.SemaphoreType.DMA((2,)),
            pltpu.SemaphoreType.DMA((2,)),
            pltpu.SemaphoreType.DMA((3 * CHUNKS,)),
            pltpu.SemaphoreType.DMA((3 * CHUNKS,)),
        ],
        compiler_params=pltpu.CompilerParams(
            collective_id=0, has_side_effects=True, vmem_limit_bytes=63 * 1024 * 1024
        ),
    )(
        key_rows,
        value_rows,
        key_kernel,
        value_kernel,
        long_filter,
        skip_gain,
        jnp.asarray(first),
        jnp.asarray(last),
        jnp.asarray(middle),
        jnp.asarray(order),
        jnp.asarray(twist),
    )


def solution(mesh):
    return jax.shard_map(
        functools.partial(on_device, mesh.shape["seq"]),
        mesh=mesh,
        in_specs=(
            P("seq", "batch"),
            P("seq", "batch"),
            P(None, "batch"),
            P(None, "batch"),
            P("seq", "batch"),
            P("batch"),
        ),
        out_specs=P("seq", "batch"),
        check_vma=False,
    )
```

```python
import functools
import math

import jax
import jax.numpy as jnp
import numpy as np
from jax import lax
from jax.experimental import pallas as pl
from jax.experimental.pallas import tpu as pltpu
from jax.sharding import PartitionSpec as P

import ml_dtypes

MESH = pl.DeviceIdType.MESH
F32 = jnp.float32
BF16 = jnp.bfloat16
CHUNKS = 4
LANES = 4
PIECES = 4


def tables(n, rows):
    length = n * rows
    piece_rows = rows // PIECES
    outer = 2.0 * math.pi * np.outer(np.arange(n) + 0.25, np.arange(n)) / n
    pair = np.stack([np.cos(outer), -np.sin(outer)])
    first = np.einsum("pks,hg,cd->hpcksgd", pair, np.eye(PIECES), np.eye(LANES))
    first = first.reshape(PIECES * 2 * LANES * n, n * PIECES * LANES)
    last = first.T
    inner = 2.0 * math.pi * (np.outer(np.arange(rows), np.arange(rows)) % rows) / rows
    c, s = np.cos(inner), np.sin(inner)
    middle = np.block([[c, -s], [s, c]])
    order = np.einsum("de,hg,cb->dhcgeb", np.eye(n), np.eye(PIECES), np.eye(LANES))
    order = order.reshape(n * PIECES * LANES, -1)
    twist = 2.0 * math.pi * np.outer(np.arange(n) + 0.25, np.arange(rows)) / length
    low = lambda a: np.ascontiguousarray(a).astype(ml_dtypes.bfloat16)
    return (
        low(first),
        low(last),
        low(middle),
        low(order),
        np.stack([np.cos(twist), np.sin(twist)]).astype(np.float32),
    )


def kernel(
    n,
    key_hbm,
    value_hbm,
    key_taps_hbm,
    value_taps_hbm,
    filter_hbm,
    skip_hbm,
    first_hbm,
    last_hbm,
    middle_hbm,
    order_hbm,
    twist_hbm,
    out,
    keys,
    values,
    filt,
    key_taps,
    value_taps,
    skip,
    first,
    last,
    middle,
    order,
    twist,
    rim,
    send,
    recv,
    spectrum,
    mixed,
    stacked,
    in_sem,
    rim_send,
    rim_recv,
    send_sem,
    recv_sem,
):
    me = lax.axis_index("seq")
    planes = n // 4
    my_side, my_plane, my_core = me // (2 * planes), (me // 2) % planes, me % 2
    rows, channels = keys.shape
    piece_rows = rows // PIECES
    width = channels // CHUNKS
    modes = LANES * n
    right = lax.rem(me + 1, n)

    barrier = pltpu.get_barrier_semaphore()

    def flip(place, other):
        return 1 - place if other else place

    def each_peer(act):
        def step(i, carry):
            shift = (i + 1) // 2
            distance = planes // 2 + jnp.where(i % 2 == 1, -shift, shift)
            plane = my_plane + distance
            plane = jnp.where(plane >= planes, plane - planes, plane)
            for side in (1, 0):
                for core in (1, 0):
                    act(flip(my_side, side) * 2 * planes + plane * 2 + flip(my_core, core))
            return carry

        lax.fori_loop(0, planes - 1, step, 0)
        for side, core in ((1, 1), (1, 0), (0, 1)):
            act(flip(my_side, side) * 2 * planes + my_plane * 2 + flip(my_core, core))

    each_peer(
        lambda peer: pl.semaphore_signal(
            barrier, inc=1, device_id={"seq": peer}, device_id_type=MESH
        )
    )

    loads = [
        pltpu.make_async_copy(source, target, in_sem.at[i])
        for i, (source, target) in enumerate(
            (
                (filter_hbm, filt),
                (order_hbm, order),
                (key_hbm, keys),
                (value_hbm, values),
                (key_taps_hbm, key_taps),
                (value_taps_hbm, value_taps),
                (skip_hbm, skip),
                (first_hbm, first),
                (twist_hbm, twist),
                (middle_hbm, middle),
                (last_hbm, last),
            )
        )
    ]
    for load in loads:
        load.start()

    def pack(slot, block):
        parts = [block[h * piece_rows : (h + 1) * piece_rows] for h in range(PIECES)]
        slabs = lax.dot_general(
            order[...],
            jnp.concatenate(parts, axis=1),
            (((1,), (1,)), ((), ())),
            preferred_element_type=F32,
        )
        send[slot] = slabs.astype(BF16).reshape(n, PIECES * LANES, piece_rows)

    def send_to(slot, peer):
        pltpu.make_async_remote_copy(
            src_ref=send.at[slot, peer],
            dst_ref=recv.at[slot, me],
            send_sem=send_sem.at[slot],
            recv_sem=recv_sem.at[slot],
            device_id={"seq": peer},
            device_id_type=MESH,
        ).start()

    def scatter(slot):
        each_peer(functools.partial(send_to, slot))
        recv[slot, pl.ds(me, 1)] = send[slot, pl.ds(me, 1)]

    def arrived(slot):
        block = recv.at[slot, pl.ds(0, n - 1)]
        pltpu.make_async_copy(block, block, recv_sem.at[slot]).wait()

    def gone(slot):
        block = send.at[slot, pl.ds(0, n - 1)]
        pltpu.make_async_copy(block, block, send_sem.at[slot]).wait()

    def turn(part, h):
        table = twist[part, :, h * piece_rows : (h + 1) * piece_rows]
        return jnp.broadcast_to(table[None], (LANES, n, piece_rows)).reshape(modes, piece_rows)

    def forward(slot):
        block = recv[slot].reshape(n * PIECES * LANES, piece_rows)
        both = jnp.dot(first[...], block, preferred_element_type=F32)
        for h in range(PIECES):
            start = 2 * h * modes
            re, im = both[start : start + modes], both[start + modes : start + 2 * modes]
            c, s = turn(0, h), turn(1, h)
            mixed[:, h * piece_rows : (h + 1) * piece_rows] = (re * c + im * s).astype(BF16)
            mixed[:, rows + h * piece_rows : rows + (h + 1) * piece_rows] = (
                im * c - re * s
            ).astype(BF16)
        both = jnp.dot(mixed[...], middle[...], preferred_element_type=F32)
        return both[:, :rows], both[:, rows:]

    loads[0].wait()
    loads[1].wait()
    pack(0, filt[:, :width])
    pl.semaphore_wait(barrier, n - 1)
    loads[2].wait()
    loads[3].wait()
    rims = [
        pltpu.make_async_remote_copy(
            src_ref=array.at[pl.ds(rows - 16, 16)],
            dst_ref=rim.at[i],
            send_sem=rim_send.at[i],
            recv_sem=rim_recv.at[i],
            device_id={"seq": right},
            device_id_type=MESH,
        )
        for i, array in enumerate((keys, values))
    ]
    for copy in rims:
        copy.start()
    scatter(0)
    for load in loads[4:6]:
        load.wait()
    for copy in rims:
        copy.wait_recv()

    def short(samples, i, taps, columns):
        behind = rim[i, :, columns].astype(F32) * (me > 0).astype(F32)
        longer = jnp.concatenate([behind[8:], samples[:, columns].astype(F32)], axis=0)
        return (
            taps[0:1, columns] * longer[8:]
            + taps[1:2, columns] * longer[7 : rows + 7]
            + taps[2:3, columns] * longer[6 : rows + 6]
        )

    for q in range(CHUNKS):
        columns = slice(q * width, (q + 1) * width)
        if q:
            pack(q, filt[:, columns])
            scatter(q)
        gated = short(keys, 0, key_taps, columns) * short(values, 1, value_taps, columns)
        pack(CHUNKS + q, gated.astype(BF16))
        scatter(CHUNKS + q)

    for load in loads[6:]:
        load.wait()
    scale = 1.0 / (n * rows)
    for q in range(CHUNKS):
        arrived(q)
        re, im = forward(q)
        for c in range(LANES):
            gain = skip[q * width + me * LANES + c]
            spectrum[0, c * n : (c + 1) * n] = (re[c * n : (c + 1) * n] + gain) * scale
        spectrum[1] = im * scale

        arrived(CHUNKS + q)
        re, im = forward(CHUNKS + q)
        fre, fim = spectrum[0], spectrum[1]
        mixed[:, :rows] = (re * fim + im * fre).astype(BF16)
        mixed[:, rows:] = (re * fre - im * fim).astype(BF16)
        both = jnp.dot(mixed[...], middle[...], preferred_element_type=F32)
        im, re = both[:, :rows], both[:, rows:]
        for h in range(PIECES):
            part = slice(h * piece_rows, (h + 1) * piece_rows)
            c, s = turn(0, h), turn(1, h)
            start = 2 * h * modes
            stacked[start : start + modes] = (re[:, part] * c - im[:, part] * s).astype(BF16)
            stacked[start + modes : start + 2 * modes] = (
                im[:, part] * c + re[:, part] * s
            ).astype(BF16)
        done = jnp.dot(last[...], stacked[...], preferred_element_type=F32)
        send[2 * CHUNKS + q] = done.astype(BF16).reshape(n, PIECES * LANES, piece_rows)
        scatter(2 * CHUNKS + q)

    for q in range(CHUNKS):
        arrived(2 * CHUNKS + q)
        block = recv[2 * CHUNKS + q].reshape(n * PIECES * LANES, piece_rows)
        turned = lax.dot_general(
            block, order[...], (((0,), (0,)), ((), ())), preferred_element_type=F32
        )
        for h in range(PIECES):
            out[h * piece_rows : (h + 1) * piece_rows, q * width : (q + 1) * width] = turned[
                :, h * width : (h + 1) * width
            ].astype(BF16)

    for copy in rims:
        copy.wait_send()
    for slot in range(3 * CHUNKS):
        gone(slot)


def on_device(n, key_rows, value_rows, key_kernel, value_kernel, long_filter, skip_gain):
    rows, channels = key_rows.shape
    piece_rows = rows // PIECES
    modes = LANES * n
    first, last, middle, order, twist = tables(n, rows)
    vmem = pl.BlockSpec(memory_space=pltpu.VMEM)
    hbm = pl.BlockSpec(memory_space=pltpu.HBM)
    slabs = (3 * CHUNKS, n, PIECES * LANES, piece_rows)
    return pl.pallas_call(
        functools.partial(kernel, n),
        out_shape=pltpu.VMEM((rows, channels), BF16),
        in_specs=[hbm] * 11,
        out_specs=vmem,
        scratch_shapes=[
            pltpu.VMEM((rows, channels), BF16),
            pltpu.VMEM((rows, channels), BF16),
            pltpu.VMEM((rows, channels), BF16),
            pltpu.VMEM(key_kernel.shape, F32),
            pltpu.VMEM(value_kernel.shape, F32),
            pltpu.SMEM(skip_gain.shape, F32),
            pltpu.VMEM(first.shape, BF16),
            pltpu.VMEM(last.shape, BF16),
            pltpu.VMEM(middle.shape, BF16),
            pltpu.VMEM(order.shape, BF16),
            pltpu.VMEM(twist.shape, F32),
            pltpu.VMEM((2, 16, channels), BF16),
            pltpu.VMEM(slabs, BF16),
            pltpu.VMEM(slabs, BF16),
            pltpu.VMEM((2, modes, rows), F32),
            pltpu.VMEM((modes, 2 * rows), BF16),
            pltpu.VMEM((2 * PIECES * modes, piece_rows), BF16),
            pltpu.SemaphoreType.DMA((11,)),
            pltpu.SemaphoreType.DMA((2,)),
            pltpu.SemaphoreType.DMA((2,)),
            pltpu.SemaphoreType.DMA((3 * CHUNKS,)),
            pltpu.SemaphoreType.DMA((3 * CHUNKS,)),
        ],
        compiler_params=pltpu.CompilerParams(
            collective_id=0, has_side_effects=True, vmem_limit_bytes=63 * 1024 * 1024
        ),
    )(
        key_rows,
        value_rows,
        key_kernel,
        value_kernel,
        long_filter,
        skip_gain,
        jnp.asarray(first),
        jnp.asarray(last),
        jnp.asarray(middle),
        jnp.asarray(order),
        jnp.asarray(twist),
    )


def solution(mesh):
    return jax.shard_map(
        functools.partial(on_device, mesh.shape["seq"]),
        mesh=mesh,
        in_specs=(
            P("seq", "batch"),
            P("seq", "batch"),
            P(None, "batch"),
            P(None, "batch"),
            P("seq", "batch"),
            P("batch"),
        ),
        out_specs=P("seq", "batch"),
        check_vma=False,
    )
```

```python
import functools
import math

import jax
import jax.numpy as jnp
import numpy as np
from jax import lax
from jax.experimental import pallas as pl
from jax.experimental.pallas import tpu as pltpu
from jax.sharding import PartitionSpec as P

import ml_dtypes

MESH = pl.DeviceIdType.MESH
F32 = jnp.float32
BF16 = jnp.bfloat16
CHUNKS = 4
LANES = 4
PIECES = 4


def tables(n, rows):
    length = n * rows
    piece_rows = rows // PIECES
    outer = 2.0 * math.pi * np.outer(np.arange(n) + 0.25, np.arange(n)) / n
    pair = np.stack([np.cos(outer), -np.sin(outer)])
    first = np.einsum("pks,hg,cd->hpcksgd", pair, np.eye(PIECES), np.eye(LANES))
    first = first.reshape(PIECES * 2 * LANES * n, n * PIECES * LANES)
    last = first.T
    inner = 2.0 * math.pi * (np.outer(np.arange(rows), np.arange(rows)) % rows) / rows
    c, s = np.cos(inner), np.sin(inner)
    middle = np.block([[c, -s], [s, c]])
    order = np.einsum("de,hg,cb->dhcgeb", np.eye(n), np.eye(PIECES), np.eye(LANES))
    order = order.reshape(n * PIECES * LANES, -1)
    twist = 2.0 * math.pi * np.outer(np.arange(n) + 0.25, np.arange(rows)) / length
    low = lambda a: np.ascontiguousarray(a).astype(ml_dtypes.bfloat16)
    return (
        low(first),
        low(last),
        low(middle),
        low(order),
        np.stack([np.cos(twist), np.sin(twist)]).astype(np.float32),
    )


def kernel(
    n,
    key_hbm,
    value_hbm,
    key_taps_hbm,
    value_taps_hbm,
    filter_hbm,
    skip_hbm,
    first_hbm,
    last_hbm,
    middle_hbm,
    order_hbm,
    twist_hbm,
    out,
    keys,
    values,
    filt,
    key_taps,
    value_taps,
    skip,
    first,
    last,
    middle,
    order,
    twist,
    rim,
    send,
    recv,
    spectrum,
    mixed,
    stacked,
    in_sem,
    rim_send,
    rim_recv,
    send_sem,
    recv_sem,
    told,
):
    me = lax.axis_index("seq")
    planes = n // 4
    my_side, my_plane, my_core = me // (2 * planes), (me // 2) % planes, me % 2
    rows, channels = keys.shape
    piece_rows = rows // PIECES
    width = channels // CHUNKS
    modes = LANES * n
    right = lax.rem(me + 1, n)

    barrier = pltpu.get_barrier_semaphore()

    def flip(place, other):
        return 1 - place if other else place

    def each_peer(act):
        def step(i, carry):
            shift = (i + 1) // 2
            distance = planes // 2 + jnp.where(i % 2 == 1, -shift, shift)
            plane = my_plane + distance
            plane = jnp.where(plane >= planes, plane - planes, plane)
            for side in (1, 0):
                for core in (1, 0):
                    act(flip(my_side, side) * 2 * planes + plane * 2 + flip(my_core, core))
            return carry

        lax.fori_loop(0, planes - 1, step, 0)
        same_plane(act)

    def at_distances(distances, act):
        for distance in distances:
            plane = my_plane + distance % planes
            plane = jnp.where(plane >= planes, plane - planes, plane)
            for side in (1, 0):
                for core in (1, 0):
                    act(flip(my_side, side) * 2 * planes + plane * 2 + flip(my_core, core))

    def same_plane(act):
        for side, core in ((1, 1), (1, 0), (0, 1)):
            act(flip(my_side, side) * 2 * planes + my_plane * 2 + flip(my_core, core))

    def column(distance):
        plane = my_plane + distance % planes
        plane = jnp.where(plane >= planes, plane - planes, plane)
        return my_side * 2 * planes + plane * 2 + my_core

    def signal(semaphore, peer):
        pl.semaphore_signal(semaphore, inc=1, device_id={"seq": peer}, device_id_type=MESH)

    near, far = (2, -2, 1, -1), (3, -3)
    at_distances(near, functools.partial(signal, barrier))
    same_plane(functools.partial(signal, barrier))

    loads = [
        pltpu.make_async_copy(source, target, in_sem.at[i])
        for i, (source, target) in enumerate(
            (
                (filter_hbm, filt),
                (order_hbm, order),
                (key_hbm, keys),
                (value_hbm, values),
                (key_taps_hbm, key_taps),
                (value_taps_hbm, value_taps),
                (skip_hbm, skip),
                (first_hbm, first),
                (twist_hbm, twist),
                (middle_hbm, middle),
                (last_hbm, last),
            )
        )
    ]
    for load in loads:
        load.start()

    def pack(slot, block):
        parts = [block[h * piece_rows : (h + 1) * piece_rows] for h in range(PIECES)]
        slabs = lax.dot_general(
            order[...],
            jnp.concatenate(parts, axis=1),
            (((1,), (1,)), ((), ())),
            preferred_element_type=F32,
        )
        send[slot] = slabs.astype(BF16).reshape(n, PIECES * LANES, piece_rows)

    def send_to(slot, peer):
        pltpu.make_async_remote_copy(
            src_ref=send.at[slot, peer],
            dst_ref=recv.at[slot, me],
            send_sem=send_sem.at[slot],
            recv_sem=recv_sem.at[slot],
            device_id={"seq": peer},
            device_id_type=MESH,
        ).start()

    def keep(slot):
        recv[slot, pl.ds(me, 1)] = send[slot, pl.ds(me, 1)]

    def scatter(slot):
        keep(slot)
        each_peer(functools.partial(send_to, slot))

    def arrived(slot):
        block = recv.at[slot, pl.ds(0, n - 1)]
        pltpu.make_async_copy(block, block, recv_sem.at[slot]).wait()

    def gone(slot):
        block = send.at[slot, pl.ds(0, n - 1)]
        pltpu.make_async_copy(block, block, send_sem.at[slot]).wait()

    def turn(part, h):
        table = twist[part, :, h * piece_rows : (h + 1) * piece_rows]
        return jnp.broadcast_to(table[None], (LANES, n, piece_rows)).reshape(modes, piece_rows)

    def forward(slot):
        block = recv[slot].reshape(n * PIECES * LANES, piece_rows)
        both = jnp.dot(first[...], block, preferred_element_type=F32)
        for h in range(PIECES):
            start = 2 * h * modes
            re, im = both[start : start + modes], both[start + modes : start + 2 * modes]
            c, s = turn(0, h), turn(1, h)
            mixed[:, h * piece_rows : (h + 1) * piece_rows] = (re * c + im * s).astype(BF16)
            mixed[:, rows + h * piece_rows : rows + (h + 1) * piece_rows] = (
                im * c - re * s
            ).astype(BF16)
        both = jnp.dot(mixed[...], middle[...], preferred_element_type=F32)
        return both[:, :rows], both[:, rows:]

    loads[0].wait()
    loads[1].wait()
    pack(0, filt[:, :width])
    pl.semaphore_wait(barrier, 4 * (len(near) + 1) - 1)
    signal(told.at[0], column(-1))
    signal(told.at[1], column(1))
    signal(told.at[2], column(-2))
    loads[2].wait()
    loads[3].wait()
    rims = [
        pltpu.make_async_remote_copy(
            src_ref=array.at[pl.ds(rows - 16, 16)],
            dst_ref=rim.at[i],
            send_sem=rim_send.at[i],
            recv_sem=rim_recv.at[i],
            device_id={"seq": right},
            device_id_type=MESH,
        )
        for i, array in enumerate((keys, values))
    ]
    for copy in rims:
        copy.start()
    keep(0)
    at_distances(near, functools.partial(send_to, 0))
    same_plane(functools.partial(send_to, 0))
    pack(1, filt[:, width : 2 * width])
    keep(1)
    at_distances(near, functools.partial(send_to, 1))
    same_plane(functools.partial(send_to, 1))
    pl.semaphore_wait(told.at[0], 1)
    at_distances(far[:1], functools.partial(send_to, 0))
    at_distances(far[:1], functools.partial(send_to, 1))
    pl.semaphore_wait(told.at[1], 1)
    at_distances(far[1:], functools.partial(send_to, 0))
    at_distances(far[1:], functools.partial(send_to, 1))
    pl.semaphore_wait(told.at[2], 1)
    at_distances((4,), functools.partial(send_to, 0))
    at_distances((4,), functools.partial(send_to, 1))
    for load in loads[4:6]:
        load.wait()
    for copy in rims:
        copy.wait_recv()

    def short(samples, i, taps, columns):
        behind = rim[i, :, columns].astype(F32) * (me > 0).astype(F32)
        longer = jnp.concatenate([behind[8:], samples[:, columns].astype(F32)], axis=0)
        return (
            taps[0:1, columns] * longer[8:]
            + taps[1:2, columns] * longer[7 : rows + 7]
            + taps[2:3, columns] * longer[6 : rows + 6]
        )

    for q in range(CHUNKS):
        columns = slice(q * width, (q + 1) * width)
        if q > 1:
            pack(q, filt[:, columns])
            scatter(q)
        gated = short(keys, 0, key_taps, columns) * short(values, 1, value_taps, columns)
        pack(CHUNKS + q, gated.astype(BF16))
        scatter(CHUNKS + q)

    for load in loads[6:]:
        load.wait()
    scale = 1.0 / (n * rows)
    for q in range(CHUNKS):
        arrived(q)
        re, im = forward(q)
        for c in range(LANES):
            gain = skip[q * width + me * LANES + c]
            spectrum[0, c * n : (c + 1) * n] = (re[c * n : (c + 1) * n] + gain) * scale
        spectrum[1] = im * scale

        arrived(CHUNKS + q)
        re, im = forward(CHUNKS + q)
        fre, fim = spectrum[0], spectrum[1]
        mixed[:, :rows] = (re * fim + im * fre).astype(BF16)
        mixed[:, rows:] = (re * fre - im * fim).astype(BF16)
        both = jnp.dot(mixed[...], middle[...], preferred_element_type=F32)
        im, re = both[:, :rows], both[:, rows:]
        for h in range(PIECES):
            part = slice(h * piece_rows, (h + 1) * piece_rows)
            c, s = turn(0, h), turn(1, h)
            start = 2 * h * modes
            stacked[start : start + modes] = (re[:, part] * c - im[:, part] * s).astype(BF16)
            stacked[start + modes : start + 2 * modes] = (
                im[:, part] * c + re[:, part] * s
            ).astype(BF16)
        done = jnp.dot(last[...], stacked[...], preferred_element_type=F32)
        send[2 * CHUNKS + q] = done.astype(BF16).reshape(n, PIECES * LANES, piece_rows)
        scatter(2 * CHUNKS + q)

    for q in range(CHUNKS):
        arrived(2 * CHUNKS + q)
        block = recv[2 * CHUNKS + q].reshape(n * PIECES * LANES, piece_rows)
        turned = lax.dot_general(
            block, order[...], (((0,), (0,)), ((), ())), preferred_element_type=F32
        )
        for h in range(PIECES):
            out[h * piece_rows : (h + 1) * piece_rows, q * width : (q + 1) * width] = turned[
                :, h * width : (h + 1) * width
            ].astype(BF16)

    for copy in rims:
        copy.wait_send()
    for slot in range(3 * CHUNKS):
        gone(slot)


def on_device(n, key_rows, value_rows, key_kernel, value_kernel, long_filter, skip_gain):
    rows, channels = key_rows.shape
    piece_rows = rows // PIECES
    modes = LANES * n
    first, last, middle, order, twist = tables(n, rows)
    vmem = pl.BlockSpec(memory_space=pltpu.VMEM)
    hbm = pl.BlockSpec(memory_space=pltpu.HBM)
    slabs = (3 * CHUNKS, n, PIECES * LANES, piece_rows)
    return pl.pallas_call(
        functools.partial(kernel, n),
        out_shape=pltpu.VMEM((rows, channels), BF16),
        in_specs=[hbm] * 11,
        out_specs=vmem,
        scratch_shapes=[
            pltpu.VMEM((rows, channels), BF16),
            pltpu.VMEM((rows, channels), BF16),
            pltpu.VMEM((rows, channels), BF16),
            pltpu.VMEM(key_kernel.shape, F32),
            pltpu.VMEM(value_kernel.shape, F32),
            pltpu.SMEM(skip_gain.shape, F32),
            pltpu.VMEM(first.shape, BF16),
            pltpu.VMEM(last.shape, BF16),
            pltpu.VMEM(middle.shape, BF16),
            pltpu.VMEM(order.shape, BF16),
            pltpu.VMEM(twist.shape, F32),
            pltpu.VMEM((2, 16, channels), BF16),
            pltpu.VMEM(slabs, BF16),
            pltpu.VMEM(slabs, BF16),
            pltpu.VMEM((2, modes, rows), F32),
            pltpu.VMEM((modes, 2 * rows), BF16),
            pltpu.VMEM((2 * PIECES * modes, piece_rows), BF16),
            pltpu.SemaphoreType.DMA((11,)),
            pltpu.SemaphoreType.DMA((2,)),
            pltpu.SemaphoreType.DMA((2,)),
            pltpu.SemaphoreType.DMA((3 * CHUNKS,)),
            pltpu.SemaphoreType.DMA((3 * CHUNKS,)),
            pltpu.SemaphoreType.REGULAR((3,)),
        ],
        compiler_params=pltpu.CompilerParams(
            collective_id=0, has_side_effects=True, vmem_limit_bytes=63 * 1024 * 1024
        ),
    )(
        key_rows,
        value_rows,
        key_kernel,
        value_kernel,
        long_filter,
        skip_gain,
        jnp.asarray(first),
        jnp.asarray(last),
        jnp.asarray(middle),
        jnp.asarray(order),
        jnp.asarray(twist),
    )


def solution(mesh):
    return jax.shard_map(
        functools.partial(on_device, mesh.shape["seq"]),
        mesh=mesh,
        in_specs=(
            P("seq", "batch"),
            P("seq", "batch"),
            P(None, "batch"),
            P(None, "batch"),
            P("seq", "batch"),
            P("batch"),
        ),
        out_specs=P("seq", "batch"),
        check_vma=False,
    )
```

```python
import functools
import math

import jax
import jax.numpy as jnp
import numpy as np
from jax import lax
from jax.experimental import pallas as pl
from jax.experimental.pallas import tpu as pltpu
from jax.sharding import PartitionSpec as P

import ml_dtypes

MESH = pl.DeviceIdType.MESH
F32 = jnp.float32
BF16 = jnp.bfloat16
CHUNKS = 4
LANES = 4
PIECES = 4


def tables(n, rows):
    length = n * rows
    piece_rows = rows // PIECES
    outer = 2.0 * math.pi * np.outer(np.arange(n) + 0.25, np.arange(n)) / n
    pair = np.stack([np.cos(outer), -np.sin(outer)])
    first = np.einsum("pks,hg,cd->hpcksgd", pair, np.eye(PIECES), np.eye(LANES))
    first = first.reshape(PIECES * 2 * LANES * n, n * PIECES * LANES)
    last = first.T
    inner = 2.0 * math.pi * (np.outer(np.arange(rows), np.arange(rows)) % rows) / rows
    c, s = np.cos(inner), np.sin(inner)
    middle = np.block([[c, -s], [s, c]])
    order = np.einsum("de,hg,cb->dhcgeb", np.eye(n), np.eye(PIECES), np.eye(LANES))
    order = order.reshape(n * PIECES * LANES, -1)
    twist = 2.0 * math.pi * np.outer(np.arange(n) + 0.25, np.arange(rows)) / length
    low = lambda a: np.ascontiguousarray(a).astype(ml_dtypes.bfloat16)
    return (
        low(first),
        low(last),
        low(middle),
        low(order),
        np.stack([np.cos(twist), np.sin(twist)]).astype(np.float32),
    )


def kernel(
    n,
    key_hbm,
    value_hbm,
    key_taps_hbm,
    value_taps_hbm,
    filter_hbm,
    skip_hbm,
    first_hbm,
    last_hbm,
    middle_hbm,
    order_hbm,
    twist_hbm,
    out,
    keys,
    values,
    filt,
    key_taps,
    value_taps,
    skip,
    first,
    last,
    middle,
    order,
    twist,
    rim,
    send,
    recv,
    spectrum,
    mixed,
    stacked,
    in_sem,
    rim_send,
    rim_recv,
    send_sem,
    recv_sem,
    told,
):
    me = lax.axis_index("seq")
    planes = n // 4
    my_side, my_plane, my_core = me // (2 * planes), (me // 2) % planes, me % 2
    rows, channels = keys.shape
    piece_rows = rows // PIECES
    width = channels // CHUNKS
    modes = LANES * n
    right = lax.rem(me + 1, n)

    barrier = pltpu.get_barrier_semaphore()

    def flip(place, other):
        return 1 - place if other else place

    def each_peer(act):
        def step(i, carry):
            shift = (i + 1) // 2
            distance = planes // 2 + jnp.where(i % 2 == 1, -shift, shift)
            plane = my_plane + distance
            plane = jnp.where(plane >= planes, plane - planes, plane)
            for side in (1, 0):
                for core in (1, 0):
                    act(flip(my_side, side) * 2 * planes + plane * 2 + flip(my_core, core))
            return carry

        lax.fori_loop(0, planes - 1, step, 0)
        same_plane(act)

    def at_distances(distances, act):
        for distance in distances:
            plane = my_plane + distance % planes
            plane = jnp.where(plane >= planes, plane - planes, plane)
            for side in (1, 0):
                for core in (1, 0):
                    act(flip(my_side, side) * 2 * planes + plane * 2 + flip(my_core, core))

    def same_plane(act):
        for side, core in ((1, 1), (1, 0), (0, 1)):
            act(flip(my_side, side) * 2 * planes + my_plane * 2 + flip(my_core, core))

    def column(distance):
        plane = my_plane + distance % planes
        plane = jnp.where(plane >= planes, plane - planes, plane)
        return my_side * 2 * planes + plane * 2 + my_core

    def signal(semaphore, peer):
        pl.semaphore_signal(semaphore, inc=1, device_id={"seq": peer}, device_id_type=MESH)

    near, far = (2, -2, 1, -1), (3, -3)
    at_distances(near, functools.partial(signal, barrier))
    same_plane(functools.partial(signal, barrier))

    loads = [
        pltpu.make_async_copy(source, target, in_sem.at[i])
        for i, (source, target) in enumerate(
            (
                (filter_hbm, filt),
                (order_hbm, order),
                (key_hbm, keys),
                (value_hbm, values),
                (key_taps_hbm, key_taps),
                (value_taps_hbm, value_taps),
                (skip_hbm, skip),
                (first_hbm, first),
                (twist_hbm, twist),
                (middle_hbm, middle),
                (last_hbm, last),
            )
        )
    ]
    for load in loads[:7]:
        load.start()

    def pack(slot, block):
        parts = [block[h * piece_rows : (h + 1) * piece_rows] for h in range(PIECES)]
        slabs = lax.dot_general(
            order[...],
            jnp.concatenate(parts, axis=1),
            (((1,), (1,)), ((), ())),
            preferred_element_type=F32,
        )
        send[slot] = slabs.astype(BF16).reshape(n, PIECES * LANES, piece_rows)

    def send_to(slot, peer):
        pltpu.make_async_remote_copy(
            src_ref=send.at[slot, peer],
            dst_ref=recv.at[slot, me],
            send_sem=send_sem.at[slot],
            recv_sem=recv_sem.at[slot],
            device_id={"seq": peer},
            device_id_type=MESH,
        ).start()

    def keep(slot):
        recv[slot, pl.ds(me, 1)] = send[slot, pl.ds(me, 1)]

    def scatter(slot):
        keep(slot)
        each_peer(functools.partial(send_to, slot))

    def arrived(slot):
        block = recv.at[slot, pl.ds(0, n - 1)]
        pltpu.make_async_copy(block, block, recv_sem.at[slot]).wait()

    def gone(slot):
        block = send.at[slot, pl.ds(0, n - 1)]
        pltpu.make_async_copy(block, block, send_sem.at[slot]).wait()

    def turn(part, h):
        table = twist[part, :, h * piece_rows : (h + 1) * piece_rows]
        return jnp.broadcast_to(table[None], (LANES, n, piece_rows)).reshape(modes, piece_rows)

    def forward(slot):
        block = recv[slot].reshape(n * PIECES * LANES, piece_rows)
        both = jnp.dot(first[...], block, preferred_element_type=F32)
        for h in range(PIECES):
            start = 2 * h * modes
            re, im = both[start : start + modes], both[start + modes : start + 2 * modes]
            c, s = turn(0, h), turn(1, h)
            mixed[:, h * piece_rows : (h + 1) * piece_rows] = (re * c + im * s).astype(BF16)
            mixed[:, rows + h * piece_rows : rows + (h + 1) * piece_rows] = (
                im * c - re * s
            ).astype(BF16)
        both = jnp.dot(mixed[...], middle[...], preferred_element_type=F32)
        return both[:, :rows], both[:, rows:]

    loads[0].wait()
    loads[1].wait()
    pack(0, filt[:, :width])
    pl.semaphore_wait(barrier, 4 * (len(near) + 1) - 1)
    signal(told.at[0], column(-1))
    signal(told.at[1], column(1))
    signal(told.at[2], column(-2))
    loads[2].wait()
    loads[3].wait()
    rims = [
        pltpu.make_async_remote_copy(
            src_ref=array.at[pl.ds(rows - 16, 16)],
            dst_ref=rim.at[i],
            send_sem=rim_send.at[i],
            recv_sem=rim_recv.at[i],
            device_id={"seq": right},
            device_id_type=MESH,
        )
        for i, array in enumerate((keys, values))
    ]
    for copy in rims:
        copy.start()
    keep(0)
    at_distances(near, functools.partial(send_to, 0))
    same_plane(functools.partial(send_to, 0))
    for load in loads[7:]:
        load.start()
    pack(1, filt[:, width : 2 * width])
    keep(1)
    at_distances(near, functools.partial(send_to, 1))
    same_plane(functools.partial(send_to, 1))
    pl.semaphore_wait(told.at[0], 1)
    at_distances(far[:1], functools.partial(send_to, 0))
    at_distances(far[:1], functools.partial(send_to, 1))
    pl.semaphore_wait(told.at[1], 1)
    at_distances(far[1:], functools.partial(send_to, 0))
    at_distances(far[1:], functools.partial(send_to, 1))
    pl.semaphore_wait(told.at[2], 1)
    at_distances((4,), functools.partial(send_to, 0))
    at_distances((4,), functools.partial(send_to, 1))
    for load in loads[4:6]:
        load.wait()
    for copy in rims:
        copy.wait_recv()

    def short(samples, i, taps, columns):
        behind = rim[i, :, columns].astype(F32) * (me > 0).astype(F32)
        longer = jnp.concatenate([behind[8:], samples[:, columns].astype(F32)], axis=0)
        return (
            taps[0:1, columns] * longer[8:]
            + taps[1:2, columns] * longer[7 : rows + 7]
            + taps[2:3, columns] * longer[6 : rows + 6]
        )

    for q in range(CHUNKS):
        columns = slice(q * width, (q + 1) * width)
        if q > 1:
            pack(q, filt[:, columns])
            scatter(q)
        gated = short(keys, 0, key_taps, columns) * short(values, 1, value_taps, columns)
        pack(CHUNKS + q, gated.astype(BF16))
        scatter(CHUNKS + q)

    for load in loads[6:]:
        load.wait()
    scale = 1.0 / (n * rows)
    for q in range(CHUNKS):
        arrived(q)
        re, im = forward(q)
        for c in range(LANES):
            gain = skip[q * width + me * LANES + c]
            spectrum[0, c * n : (c + 1) * n] = (re[c * n : (c + 1) * n] + gain) * scale
        spectrum[1] = im * scale

        arrived(CHUNKS + q)
        re, im = forward(CHUNKS + q)
        fre, fim = spectrum[0], spectrum[1]
        mixed[:, :rows] = (re * fim + im * fre).astype(BF16)
        mixed[:, rows:] = (re * fre - im * fim).astype(BF16)
        both = jnp.dot(mixed[...], middle[...], preferred_element_type=F32)
        im, re = both[:, :rows], both[:, rows:]
        for h in range(PIECES):
            part = slice(h * piece_rows, (h + 1) * piece_rows)
            c, s = turn(0, h), turn(1, h)
            start = 2 * h * modes
            stacked[start : start + modes] = (re[:, part] * c - im[:, part] * s).astype(BF16)
            stacked[start + modes : start + 2 * modes] = (
                im[:, part] * c + re[:, part] * s
            ).astype(BF16)
        done = jnp.dot(last[...], stacked[...], preferred_element_type=F32)
        send[2 * CHUNKS + q] = done.astype(BF16).reshape(n, PIECES * LANES, piece_rows)
        scatter(2 * CHUNKS + q)

    for q in range(CHUNKS):
        arrived(2 * CHUNKS + q)
        block = recv[2 * CHUNKS + q].reshape(n * PIECES * LANES, piece_rows)
        turned = lax.dot_general(
            block, order[...], (((0,), (0,)), ((), ())), preferred_element_type=F32
        )
        for h in range(PIECES):
            out[h * piece_rows : (h + 1) * piece_rows, q * width : (q + 1) * width] = turned[
                :, h * width : (h + 1) * width
            ].astype(BF16)

    for copy in rims:
        copy.wait_send()
    for slot in range(3 * CHUNKS):
        gone(slot)


def on_device(n, key_rows, value_rows, key_kernel, value_kernel, long_filter, skip_gain):
    rows, channels = key_rows.shape
    piece_rows = rows // PIECES
    modes = LANES * n
    first, last, middle, order, twist = tables(n, rows)
    vmem = pl.BlockSpec(memory_space=pltpu.VMEM)
    hbm = pl.BlockSpec(memory_space=pltpu.HBM)
    slabs = (3 * CHUNKS, n, PIECES * LANES, piece_rows)
    return pl.pallas_call(
        functools.partial(kernel, n),
        out_shape=pltpu.VMEM((rows, channels), BF16),
        in_specs=[hbm] * 11,
        out_specs=vmem,
        scratch_shapes=[
            pltpu.VMEM((rows, channels), BF16),
            pltpu.VMEM((rows, channels), BF16),
            pltpu.VMEM((rows, channels), BF16),
            pltpu.VMEM(key_kernel.shape, F32),
            pltpu.VMEM(value_kernel.shape, F32),
            pltpu.SMEM(skip_gain.shape, F32),
            pltpu.VMEM(first.shape, BF16),
            pltpu.VMEM(last.shape, BF16),
            pltpu.VMEM(middle.shape, BF16),
            pltpu.VMEM(order.shape, BF16),
            pltpu.VMEM(twist.shape, F32),
            pltpu.VMEM((2, 16, channels), BF16),
            pltpu.VMEM(slabs, BF16),
            pltpu.VMEM(slabs, BF16),
            pltpu.VMEM((2, modes, rows), F32),
            pltpu.VMEM((modes, 2 * rows), BF16),
            pltpu.VMEM((2 * PIECES * modes, piece_rows), BF16),
            pltpu.SemaphoreType.DMA((11,)),
            pltpu.SemaphoreType.DMA((2,)),
            pltpu.SemaphoreType.DMA((2,)),
            pltpu.SemaphoreType.DMA((3 * CHUNKS,)),
            pltpu.SemaphoreType.DMA((3 * CHUNKS,)),
            pltpu.SemaphoreType.REGULAR((3,)),
        ],
        compiler_params=pltpu.CompilerParams(
            collective_id=0, has_side_effects=True, vmem_limit_bytes=63 * 1024 * 1024
        ),
    )(
        key_rows,
        value_rows,
        key_kernel,
        value_kernel,
        long_filter,
        skip_gain,
        jnp.asarray(first),
        jnp.asarray(last),
        jnp.asarray(middle),
        jnp.asarray(order),
        jnp.asarray(twist),
    )


def solution(mesh):
    return jax.shard_map(
        functools.partial(on_device, mesh.shape["seq"]),
        mesh=mesh,
        in_specs=(
            P("seq", "batch"),
            P("seq", "batch"),
            P(None, "batch"),
            P(None, "batch"),
            P("seq", "batch"),
            P("batch"),
        ),
        out_specs=P("seq", "batch"),
        check_vma=False,
    )
```
